768 devices in a mesh: row: 96 (over z_hi, y, x), col: 8 (over z_lo, core).
Axes of the slice: x: 4, y: 8, z: 12 (z_hi: 3, z_lo: 4; z = z_hi * 4 + z_lo), core: 2. Of those that a mesh axis runs over, the one named last changes fastest.
Arguments:
- amplitudes: bfloat16 [49152, 16384], P('row', 'col'), may hold values from -6 to 6
- factors: bfloat16 [768, 16384], P('row', 'col'), may hold values from -0.046875 to 0.046875
- pair_mask: int32 [384, 128], P('row', 'col'), may hold values 0 or 1
- factor_mask: int32 [96, 128], P('row', 'col'), may hold values 0 or 1
Outputs:
- ladder: bfloat16 [49152, 16384], P('row', 'col')
The draws below stay inside these ranges and needn't reach their ends.
All inputs are finite; a program needn't handle non-finite values. No bound on the sum of `pair_mask` or of `factor_mask` on one device may be relied on, other than what follows from the above.
Results may differ from the reference program's by a relative error of at most 0.0048.
Values may be sent and summed in bfloat16 or wider, within the bound.
No kernel may reach another device: no remote copies, remote signals or barrier semaphores. Data moves between devices by JAX's collectives and lax.ppermute only.
A program may use at most 32 MiB of HBM per device.

```python
import jax
import jax.numpy as jnp

TILE = 128
Q_DEV = 8
NP = 49152
NV = 16384
NQ = 768
N_ROW = 96


def plant(result, stream_key, low, high):
    dims = result.shape
    place = [jax.random.randint(jax.random.fold_in(stream_key, axis), (), 0, dims[axis]) for axis in range(len(dims))]
    result = result.at[tuple(place)].set(low)
    longest = dims.index(max(dims))
    place[longest] = (place[longest] + 1) % dims[longest]
    return result.at[tuple(place)].set(high)


def block_scale(key, dims, shards, smallest, largest):
    def one(dim, parts):
        steps = jax.random.uniform(jax.random.fold_in(jax.random.fold_in(key, 6), dim), (parts,), jnp.float32, smallest / len(shards), largest / len(shards))
        return jnp.repeat(jnp.exp(steps), dims[dim] // parts).reshape((-1,) + (1,) * (len(dims) - dim - 1))

    gain = one(*shards[0])
    for cut in shards[1:]:
        gain = gain * one(*cut)
    return gain


def normal_values(stream_key, extent, width, most, split=(), dtype=jnp.bfloat16):
    factor_of = block_scale(stream_key, extent, split, -0.22, 0.18) if split else 1.0
    array = jax.random.normal(stream_key, extent, jnp.float32) * width * factor_of
    return jnp.minimum(jnp.maximum(array, -most), most).astype(dtype)


def setup_inputs(seed: int = 0) -> dict:
    seeds = jax.random.split(jax.random.key(seed), 5)
    return {
        "amplitudes": normal_values(seeds[0], (NP, NV), 1.0, 6.0, ((0, 96), (1, 8))),
        "factors": normal_values(seeds[1], (NQ, NV), NV ** -0.5, 0.046875, ((0, 96), (1, 8))),
        "pair_mask": plant((jax.random.randint(seeds[2], (NP // TILE, NV // TILE), 0, 4) < 3).astype(jnp.int32), jax.random.fold_in(seeds[2], 1), 0, 1),
        "factor_mask": plant((jax.random.randint(seeds[3], (N_ROW, NV // TILE), 0, 4) < 3).astype(jnp.int32), jax.random.fold_in(seeds[3], 1), 0, 1),
    }


def expand_mask(mask, rows, cols):
    return jnp.repeat(jnp.repeat(mask, rows, axis=0), cols, axis=1).astype(jnp.bfloat16)


def reference(amplitudes, factors, pair_mask, factor_mask):
    domain = expand_mask(pair_mask, TILE, TILE)
    masked_amps = amplitudes * domain
    masked_factor = factors * expand_mask(factor_mask, Q_DEV, TILE)
    half_ladder = jnp.dot(masked_amps, masked_factor.T, preferred_element_type=jnp.float32).astype(jnp.bfloat16)
    full_sum = jnp.dot(half_ladder, masked_factor, preferred_element_type=jnp.float32)
    return (full_sum * domain.astype(jnp.float32)).astype(jnp.bfloat16)
```

```python
import jax
import jax.numpy as jnp
from jax import lax
from jax.sharding import Mesh, PartitionSpec as P

TILE = 128
N_ZHI, N_Y, N_X, N_ZLO, N_CORE = 3, 8, 4, 4, 2
CONTRACT = (((1,), (1,)), ((), ()))


def expand_mask(mask, rows, cols):
    return jnp.repeat(jnp.repeat(mask, rows, axis=0), cols, axis=1).astype(jnp.bfloat16)


def shift(count, by):
    return [(i, (i + by) % count) for i in range(count)]


def gather_zx(block):
    peers = N_ZHI * N_X
    copies = jnp.broadcast_to(block[None], (peers, *block.shape))
    got = lax.all_to_all(copies, ("zhi", "x"), 0, 0, tiled=True)
    return got.reshape(peers * block.shape[0], block.shape[1])


def ring_y(block):
    up = down = block
    parts = [block]
    for _ in range(N_Y // 2 - 1):
        up = lax.ppermute(up, "y", shift(N_Y, 1))
        down = lax.ppermute(down, "y", shift(N_Y, -1))
        parts += [up, down]
    half = block.shape[0] // 2
    parts.append(lax.ppermute(up[:half], "y", shift(N_Y, 1)))
    parts.append(lax.ppermute(down[half:], "y", shift(N_Y, -1)))
    return parts


def sum_over_columns(partial):
    rows = partial.shape[0] // N_CORE
    core = lax.axis_index("core")
    mine = lax.dynamic_slice_in_dim(partial, core * rows, rows)
    other = lax.dynamic_slice_in_dim(partial, (1 - core) * rows, rows)
    chip = mine + lax.ppermute(other, "core", shift(N_CORE, 1))
    pieces = lax.all_to_all(chip.astype(jnp.bfloat16), "zlo", 0, 0, tiled=True)
    pieces = pieces.reshape(N_ZLO, rows // N_ZLO, -1)
    total = jnp.sum(pieces.astype(jnp.float32), axis=0).astype(jnp.bfloat16)
    half = lax.all_gather(total, "zlo", axis=0, tiled=True)
    return lax.all_gather(half, "core", axis=0, tiled=True)


def body(amplitudes, factors, pair_mask, factor_mask):
    domain = expand_mask(pair_mask, TILE, TILE)
    masked_amps = amplitudes * domain
    masked_factor = factors * expand_mask(factor_mask, factors.shape[0], TILE)
    parts = ring_y(gather_zx(masked_factor))
    gathered = jnp.concatenate(parts, axis=0)
    partial_sum = lax.dot_general(
        masked_amps, gathered, CONTRACT, preferred_element_type=jnp.float32
    )
    half_ladder = sum_over_columns(partial_sum)
    full_sum = jnp.dot(half_ladder, gathered, preferred_element_type=jnp.float32)
    return (full_sum * domain.astype(jnp.float32)).astype(jnp.bfloat16)


def solution(mesh):
    fine = Mesh(
        mesh.devices.reshape(N_ZHI, N_Y, N_X, N_ZLO, N_CORE),
        ("zhi", "y", "x", "zlo", "core"),
    )
    spec = P(("zhi", "y", "x"), ("zlo", "core"))
    return jax.shard_map(
        body, mesh=fine, in_specs=(spec,) * 4, out_specs=spec, check_vma=False
    )
```

```python
import jax
import jax.numpy as jnp
from jax import lax
from jax.sharding import Mesh, PartitionSpec as P

TILE = 128
N_ZHI, N_Y, N_X, N_ZLO, N_CORE = 3, 8, 4, 4, 2


def expand_mask(mask, rows, cols):
    return jnp.repeat(jnp.repeat(mask, rows, axis=0), cols, axis=1).astype(jnp.bfloat16)


def shift(count, by):
    return [(i, (i + by) % count) for i in range(count)]


def gather_zy(block):
    peers = N_ZHI * N_Y
    copies = jnp.broadcast_to(block[None], (peers, *block.shape))
    got = lax.all_to_all(copies, ("zhi", "y"), 0, 0, tiled=True)
    return got.reshape(peers * block.shape[0], block.shape[1])


def ring_x(block):
    up = lax.ppermute(block, "x", shift(N_X, 1))
    down = lax.ppermute(block, "x", shift(N_X, -1))
    half = block.shape[0] // 2
    far_up = lax.ppermute(up[:half], "x", shift(N_X, 1))
    far_down = lax.ppermute(down[half:], "x", shift(N_X, -1))
    return [block, up, down, far_up, far_down]


def sum_over_columns(partial):
    rows = partial.shape[0] // N_CORE
    core = lax.axis_index("core")
    mine = lax.dynamic_slice_in_dim(partial, core * rows, rows)
    other = lax.dynamic_slice_in_dim(partial, (1 - core) * rows, rows)
    chip = mine + lax.ppermute(other, "core", shift(N_CORE, 1))
    pieces = lax.all_to_all(chip.astype(jnp.bfloat16), "zlo", 0, 0, tiled=True)
    pieces = pieces.reshape(N_ZLO, rows // N_ZLO, -1)
    total = jnp.sum(pieces.astype(jnp.float32), axis=0).astype(jnp.bfloat16)
    half = lax.all_gather(total, "zlo", axis=0, tiled=True)
    return lax.all_gather(half, "core", axis=0, tiled=True)


def body(amplitudes, factors, pair_mask, factor_mask):
    domain = expand_mask(pair_mask, TILE, TILE)
    masked_amps = amplitudes * domain
    masked_factor = factors * expand_mask(factor_mask, factors.shape[0], TILE)
    block = gather_zy(masked_factor)
    block, masked_amps = lax.optimization_barrier((block, masked_amps))
    parts = ring_x(block)
    partial_sum = jnp.concatenate(
        [
            lax.dot_general(
                part,
                masked_amps,
                (((1,), (1,)), ((), ())),
                preferred_element_type=jnp.float32,
            )
            for part in parts
        ],
        axis=0,
    )
    half_ladder = sum_over_columns(partial_sum)
    gathered = jnp.concatenate(parts, axis=0)
    full_sum = lax.dot_general(
        half_ladder,
        gathered,
        (((0,), (0,)), ((), ())),
        preferred_element_type=jnp.float32,
    )
    return (full_sum * domain.astype(jnp.float32)).astype(jnp.bfloat16)


def solution(mesh):
    fine = Mesh(
        mesh.devices.reshape(N_ZHI, N_Y, N_X, N_ZLO, N_CORE),
        ("zhi", "y", "x", "zlo", "core"),
    )
    spec = P(("zhi", "y", "x"), ("zlo", "core"))
    return jax.shard_map(
        body, mesh=fine, in_specs=(spec,) * 4, out_specs=spec, check_vma=False
    )
```

```python
import jax
import jax.numpy as jnp
from jax import lax
from jax.experimental import pallas as pl
from jax.experimental.pallas import tpu as pltpu
from jax.sharding import Mesh, PartitionSpec as P

TILE = 128
N_ZHI, N_Y, N_X, N_ZLO, N_CORE = 3, 8, 4, 4, 2
PLANE = ("yhi", "ylo", "xhi", "xlo")
WIDE = 256


def expand_mask(mask, rows, cols):
    return jnp.repeat(jnp.repeat(mask, rows, axis=0), cols, axis=1).astype(jnp.bfloat16)


def shift(count, by):
    return [(i, (i + by) % count) for i in range(count)]


def from_offset(dy, dx):
    pairs = []
    for y in range(N_Y):
        for x in range(N_X):
            source = ((y + dy) % N_Y) * N_X + (x + dx) % N_X
            pairs.append((source, y * N_X + x))
    return pairs


def gather_class(block):
    axes = ("zhi", "yhi", "xhi")
    peers = N_ZHI * (N_Y // 2) * (N_X // 2)
    copies = jnp.broadcast_to(block[None], (peers, *block.shape))
    got = lax.all_to_all(copies, axes, 0, 0, tiled=True)
    return got.reshape(peers * block.shape[0], block.shape[1])


def gather_others(block):
    return [
        lax.ppermute(block, PLANE, from_offset(*offset))
        for offset in ((-1, -1), (0, 1), (1, 0))
    ]


def sum_over_columns(partial):
    rows = partial.shape[0] // N_CORE
    core = lax.axis_index("core")
    mine = lax.dynamic_slice_in_dim(partial, core * rows, rows)
    other = lax.dynamic_slice_in_dim(partial, (1 - core) * rows, rows)
    chip = mine + lax.ppermute(other, "core", shift(N_CORE, 1))
    pieces = lax.all_to_all(chip.astype(jnp.bfloat16), "zlo", 0, 0, tiled=True)
    pieces = pieces.reshape(N_ZLO, rows // N_ZLO, -1)
    total = jnp.sum(pieces.astype(jnp.float32), axis=0).astype(jnp.bfloat16)
    half = lax.all_gather(total, "zlo", axis=0, tiled=True)
    return lax.all_gather(half, "core", axis=0, tiled=True)


def expand_kernel(mask_ref, half_ref, *rest):
    *part_refs, out_ref, turned = rest
    step = pl.program_id(0)

    @pl.when(step == 0)
    def _():
        turned[...] = half_ref[...].T

    factor = jnp.concatenate([part[...] for part in part_refs], axis=0)
    full = jnp.dot(turned[...], factor, preferred_element_type=jnp.float32)
    for i in range(out_ref.shape[0] // TILE):
        for j in range(WIDE // TILE):
            keep = mask_ref[i, step * (WIDE // TILE) + j].astype(jnp.float32)
            rows, cols = pl.ds(i * TILE, TILE), pl.ds(j * TILE, TILE)
            tile = full[i * TILE : (i + 1) * TILE, j * TILE : (j + 1) * TILE]
            out_ref[rows, cols] = (tile * keep).astype(out_ref.dtype)


def expand_half(pair_mask, half, parts):
    depth, rows = half.shape
    width = parts[0].shape[1]
    return pl.pallas_call(
        expand_kernel,
        out_shape=jax.ShapeDtypeStruct((rows, width), jnp.bfloat16),
        grid=(width // WIDE,),
        in_specs=[
            pl.BlockSpec(memory_space=pltpu.SMEM),
            pl.BlockSpec((depth, rows), lambda i: (0, 0)),
        ]
        + [pl.BlockSpec((part.shape[0], WIDE), lambda i: (0, i)) for part in parts],
        out_specs=pl.BlockSpec((rows, WIDE), lambda i: (0, i)),
        scratch_shapes=[pltpu.VMEM((rows, depth), jnp.bfloat16)],
        cost_estimate=pl.CostEstimate(
            flops=2 * rows * depth * width,
            bytes_accessed=2 * (rows * depth + depth * width + rows * width),
            transcendentals=0,
        ),
        compiler_params=pltpu.CompilerParams(vmem_limit_bytes=16 * 1024 * 1024),
    )(pair_mask, half, *parts)


def body(amplitudes, factors, pair_mask, factor_mask):
    domain = expand_mask(pair_mask, TILE, TILE)
    masked_amps = amplitudes * domain
    masked_factor = factors * expand_mask(factor_mask, factors.shape[0], TILE)
    block = gather_class(masked_factor)
    block, masked_amps = lax.optimization_barrier((block, masked_amps))
    parts = [block] + gather_others(block)
    partial_sum = jnp.concatenate(
        [
            lax.dot_general(
                part,
                masked_amps,
                (((1,), (1,)), ((), ())),
                preferred_element_type=jnp.float32,
            )
            for part in parts
        ],
        axis=0,
    )
    return expand_half(pair_mask, sum_over_columns(partial_sum), parts)


def solution(mesh):
    fine = Mesh(
        mesh.devices.reshape(N_ZHI, N_Y // 2, 2, N_X // 2, 2, N_ZLO, N_CORE),
        ("zhi", *PLANE, "zlo", "core"),
    )
    spec = P(("zhi", *PLANE), ("zlo", "core"))
    return jax.shard_map(
        body, mesh=fine, in_specs=(spec,) * 4, out_specs=spec, check_vma=False
    )
```

```python
import jax
import jax.numpy as jnp
from jax import lax
from jax.experimental import pallas as pl
from jax.experimental.pallas import tpu as pltpu
from jax.sharding import PartitionSpec as P

TILE = 128
N_ZHI, N_Y, N_X, N_ZLO, N_CORE = 3, 8, 4, 4, 2
WIDE = 256
CLASS = ((0, 0), (2, 2), (4, 0), (6, 2))
OFFSETS = ((1, 1), (1, -1), (-2, 0), (0, 1), (0, -1), (1, 0), (-1, 0))
LINES = [[z * N_CORE + c for z in range(N_ZLO)] for c in range(N_CORE)]
CHIPS = [[z * N_CORE + c for c in range(N_CORE)] for z in range(N_ZLO)]


def row_index(z, y, x):
    return (z * N_Y + y % N_Y) * N_X + x % N_X


def class_groups():
    groups, seen = [], set()
    for y in range(N_Y):
        for x in range(N_X):
            group = [
                row_index(z, y + dy, x + dx) for z in range(N_ZHI) for dy, dx in CLASS
            ]
            group.sort()
            if group[0] not in seen:
                seen.add(group[0])
                groups.append(group)
    return groups


def from_offset(dy, dx):
    return [
        (row_index(z, y + dy, x + dx), row_index(z, y, x))
        for z in range(N_ZHI)
        for y in range(N_Y)
        for x in range(N_X)
    ]


def expand_mask(mask, rows, cols):
    return jnp.repeat(jnp.repeat(mask, rows, axis=0), cols, axis=1).astype(jnp.bfloat16)


def gather_class(block):
    peers = N_ZHI * len(CLASS)
    copies = jnp.broadcast_to(block[None], (peers, *block.shape))
    got = lax.all_to_all(
        copies, "row", 0, 0, axis_index_groups=class_groups(), tiled=True
    )
    return got.reshape(peers * block.shape[0], block.shape[1])


def product(part, amps):
    return lax.dot_general(
        part, amps, (((1,), (1,)), ((), ())), preferred_element_type=jnp.float32
    )


def sum_over_columns(sent, kept):
    swap = [(z * N_CORE + c, z * N_CORE + 1 - c) for z in range(N_ZLO) for c in (0, 1)]
    chip = (kept + lax.ppermute(sent, "col", swap)).astype(jnp.bfloat16)
    pieces = lax.all_to_all(chip, "col", 0, 0, axis_index_groups=LINES, tiled=True)
    pieces = pieces.reshape(N_ZLO, chip.shape[0] // N_ZLO, -1)
    total = jnp.sum(pieces.astype(jnp.float32), axis=0).astype(jnp.bfloat16)
    half = lax.all_gather(total, "col", axis=0, axis_index_groups=LINES, tiled=True)
    return lax.all_gather(half, "col", axis=0, axis_index_groups=CHIPS, tiled=True)


def expand_kernel(mask_ref, half_ref, *rest):
    *part_refs, out_ref, turned = rest
    step = pl.program_id(0)

    @pl.when(step == 0)
    def _():
        turned[...] = half_ref[...].T

    cols = pl.ds(pl.multiple_of(step * WIDE, WIDE), WIDE)
    factor = jnp.concatenate([part[:, cols] for part in part_refs], axis=0)
    full = jnp.dot(turned[...], factor, preferred_element_type=jnp.float32)
    for i in range(out_ref.shape[0] // TILE):
        for j in range(WIDE // TILE):
            keep = mask_ref[i, step * (WIDE // TILE) + j].astype(jnp.float32)
            rows, cols = pl.ds(i * TILE, TILE), pl.ds(j * TILE, TILE)
            tile = full[i * TILE : (i + 1) * TILE, j * TILE : (j + 1) * TILE]
            out_ref[rows, cols] = (tile * keep).astype(out_ref.dtype)


def expand_half(pair_mask, half, parts):
    depth, rows = half.shape
    width = parts[0].shape[1]
    whole = pl.BlockSpec(memory_space=pltpu.VMEM)
    return pl.pallas_call(
        expand_kernel,
        out_shape=jax.ShapeDtypeStruct((rows, width), jnp.bfloat16),
        grid=(width // WIDE,),
        in_specs=[pl.BlockSpec(memory_space=pltpu.SMEM), whole] + [whole] * len(parts),
        out_specs=pl.BlockSpec((rows, WIDE), lambda i: (0, i)),
        scratch_shapes=[pltpu.VMEM((rows, depth), jnp.bfloat16)],
        cost_estimate=pl.CostEstimate(
            flops=2 * rows * depth * width,
            bytes_accessed=2 * (rows * depth + depth * width + rows * width),
            transcendentals=0,
        ),
        compiler_params=pltpu.CompilerParams(vmem_limit_bytes=24 * 1024 * 1024),
    )(pair_mask, half, *parts)


def body(amplitudes, factors, pair_mask, factor_mask):
    domain = expand_mask(pair_mask, TILE, TILE)
    masked_amps = amplitudes * domain
    masked_factor = factors * expand_mask(factor_mask, factors.shape[0], TILE)
    block = gather_class(masked_factor)
    block, masked_amps = lax.optimization_barrier((block, masked_amps))
    parts = [block] + [
        lax.ppermute(block, "row", from_offset(*offset)) for offset in OFFSETS
    ]
    even, odd = parts[0::2], parts[1::2]
    first = lax.axis_index("col") % N_CORE == 0
    sent = [product(jnp.where(first, o, e), masked_amps) for e, o in zip(even, odd)]
    kept = [product(jnp.where(first, e, o), masked_amps) for e, o in zip(even, odd)]
    half = sum_over_columns(
        jnp.concatenate(sent, axis=0), jnp.concatenate(kept, axis=0)
    )
    return expand_half(pair_mask, half, even + odd)


def solution(mesh):
    spec = P("row", "col")
    return jax.shard_map(
        body, mesh=mesh, in_specs=(spec,) * 4, out_specs=spec, check_vma=False
    )
```

```python
import jax
import jax.numpy as jnp
from jax import lax
from jax.experimental import pallas as pl
from jax.experimental.pallas import tpu as pltpu
from jax.sharding import PartitionSpec as P

TILE = 128
N_ZHI, N_Y, N_X, N_ZLO, N_CORE = 3, 8, 4, 4, 2
WIDE = 512
CLASS = ((0, 0), (2, 2), (4, 0), (6, 2))
LINES = [[z * N_CORE + c for z in range(N_ZLO)] for c in range(N_CORE)]
CHIPS = [[z * N_CORE + c for c in range(N_CORE)] for z in range(N_ZLO)]


def row_index(z, y, x):
    return (z * N_Y + y % N_Y) * N_X + x % N_X


def class_groups():
    groups, seen = [], set()
    for y in range(N_Y):
        for x in range(N_X):
            group = [
                row_index(z, y + dy, x + dx) for z in range(N_ZHI) for dy, dx in CLASS
            ]
            group.sort()
            if group[0] not in seen:
                seen.add(group[0])
                groups.append(group)
    return groups


def fetch(block, dy, dx):
    pairs = [
        (row_index(z, y + dy, x + dx), row_index(z, y, x))
        for z in range(N_ZHI)
        for y in range(N_Y)
        for x in range(N_X)
    ]
    return lax.ppermute(block, "row", pairs)


def expand_mask(mask, rows, cols):
    return jnp.repeat(jnp.repeat(mask, rows, axis=0), cols, axis=1).astype(jnp.bfloat16)


def gather_class(block):
    peers = N_ZHI * len(CLASS)
    copies = jnp.broadcast_to(block[None], (peers, *block.shape))
    got = lax.all_to_all(
        copies, "row", 0, 0, axis_index_groups=class_groups(), tiled=True
    )
    return got.reshape(peers * block.shape[0], block.shape[1])


def product(part, amps):
    return lax.dot_general(
        part, amps, (((1,), (1,)), ((), ())), preferred_element_type=jnp.float32
    )


def sum_over_columns(sent, kept):
    swap = [(z * N_CORE + c, z * N_CORE + 1 - c) for z in range(N_ZLO) for c in (0, 1)]
    chip = (kept + lax.ppermute(sent, "col", swap)).astype(jnp.bfloat16)
    pieces = lax.all_to_all(chip, "col", 0, 0, axis_index_groups=LINES, tiled=True)
    pieces = pieces.reshape(N_ZLO, chip.shape[0] // N_ZLO, -1)
    total = jnp.sum(pieces.astype(jnp.float32), axis=0).astype(jnp.bfloat16)
    copies = jnp.broadcast_to(total[None], (N_ZLO, *total.shape))
    half = lax.all_to_all(copies, "col", 0, 0, axis_index_groups=LINES, tiled=True)
    half = half.reshape(chip.shape)
    return lax.all_gather(half, "col", axis=0, axis_index_groups=CHIPS, tiled=True)


def expand_kernel(mask_ref, half_ref, *rest):
    *part_refs, out_ref = rest
    step = pl.program_id(0)
    cols = pl.ds(pl.multiple_of(step * WIDE, WIDE), WIDE)
    factor = jnp.concatenate([part[:, cols] for part in part_refs], axis=0)
    full = lax.dot_general(
        half_ref[...],
        factor,
        (((0,), (0,)), ((), ())),
        preferred_element_type=jnp.float32,
    )
    for i in range(out_ref.shape[0] // TILE):
        for j in range(WIDE // TILE):
            keep = mask_ref[i, step * (WIDE // TILE) + j].astype(jnp.float32)
            rows, cols = pl.ds(i * TILE, TILE), pl.ds(j * TILE, TILE)
            tile = full[i * TILE : (i + 1) * TILE, j * TILE : (j + 1) * TILE]
            out_ref[rows, cols] = (tile * keep).astype(out_ref.dtype)


def expand_half(pair_mask, half, parts):
    depth, rows = half.shape
    width = parts[0].shape[1]
    whole = pl.BlockSpec(memory_space=pltpu.VMEM)
    return pl.pallas_call(
        expand_kernel,
        out_shape=jax.ShapeDtypeStruct((rows, width), jnp.bfloat16),
        grid=(width // WIDE,),
        in_specs=[pl.BlockSpec(memory_space=pltpu.SMEM), whole] + [whole] * len(parts),
        out_specs=pl.BlockSpec((rows, WIDE), lambda i: (0, i)),
        cost_estimate=pl.CostEstimate(
            flops=2 * rows * depth * width,
            bytes_accessed=2 * (rows * depth + depth * width + rows * width),
            transcendentals=0,
        ),
        compiler_params=pltpu.CompilerParams(vmem_limit_bytes=24 * 1024 * 1024),
    )(pair_mask, half, *parts)


def body(amplitudes, factors, pair_mask, factor_mask):
    domain = expand_mask(pair_mask, TILE, TILE)
    masked_amps = amplitudes * domain
    masked_factor = factors * expand_mask(factor_mask, factors.shape[0], TILE)
    block = gather_class(masked_factor)
    block, masked_amps = lax.optimization_barrier((block, masked_amps))
    right = fetch(block, 0, 1)
    left = fetch(block, 0, -1)
    both = jnp.concatenate([block, right], axis=0)
    below = fetch(both, 1, 0)
    above = fetch(both, -1, 0)
    far = fetch(right, 0, 1)
    even, odd = [block, below, left], [right, above, far]
    first = lax.axis_index("col") % N_CORE == 0
    sent = [product(jnp.where(first, o, e), masked_amps) for e, o in zip(even, odd)]
    kept = [product(jnp.where(first, e, o), masked_amps) for e, o in zip(even, odd)]
    sent, kept[0], kept[2] = lax.optimization_barrier(
        (jnp.concatenate(sent, axis=0), kept[0], kept[2])
    )
    kept = jnp.concatenate(kept, axis=0)
    return expand_half(pair_mask, sum_over_columns(sent, kept), even + odd)


def solution(mesh):
    spec = P("row", "col")
    return jax.shard_map(
        body, mesh=mesh, in_specs=(spec,) * 4, out_specs=spec, check_vma=False
    )
```

```python
import jax
import jax.numpy as jnp
from jax import lax
from jax.experimental import pallas as pl
from jax.experimental.pallas import tpu as pltpu
from jax.sharding import PartitionSpec as P

TILE = 128
N_ZHI, N_Y, N_X, N_ZLO, N_CORE = 3, 8, 4, 4, 2
WIDE = 512
CLASS = ((0, 0), (2, 2), (4, 0), (6, 2))
LINES = [[z * N_CORE + c for z in range(N_ZLO)] for c in range(N_CORE)]
CHIPS = [[z * N_CORE + c for c in range(N_CORE)] for z in range(N_ZLO)]


def row_index(z, y, x):
    return (z * N_Y + y % N_Y) * N_X + x % N_X


def class_groups():
    groups, seen = [], set()
    for y in range(N_Y):
        for x in range(N_X):
            group = [
                row_index(z, y + dy, x + dx) for z in range(N_ZHI) for dy, dx in CLASS
            ]
            group.sort()
            if group[0] not in seen:
                seen.add(group[0])
                groups.append(group)
    return groups


def fetch(block, dy, dx):
    pairs = [
        (row_index(z, y + dy, x + dx), row_index(z, y, x))
        for z in range(N_ZHI)
        for y in range(N_Y)
        for x in range(N_X)
    ]
    return lax.ppermute(block, "row", pairs)


def expand_mask(mask, rows, cols):
    return jnp.repeat(jnp.repeat(mask, rows, axis=0), cols, axis=1).astype(jnp.bfloat16)


def gather_class(factors, factor_mask):
    copies = masked_copies(factors, factor_mask, N_ZHI * len(CLASS))
    got = lax.all_to_all(
        copies, "row", 0, 0, axis_index_groups=class_groups(), tiled=True
    )
    return got.reshape(-1, factors.shape[1])


def product(part, amps):
    return lax.dot_general(
        part, amps, (((1,), (1,)), ((), ())), preferred_element_type=jnp.float32
    )


def sum_over_columns(sent, kept):
    swap = [(z * N_CORE + c, z * N_CORE + 1 - c) for z in range(N_ZLO) for c in (0, 1)]
    chip = (kept + lax.ppermute(sent, "col", swap)).astype(jnp.bfloat16)
    pieces = lax.all_to_all(chip, "col", 0, 0, axis_index_groups=LINES, tiled=True)
    pieces = pieces.reshape(N_ZLO, chip.shape[0] // N_ZLO, -1)
    total = jnp.sum(pieces.astype(jnp.float32), axis=0).astype(jnp.bfloat16)
    copies = jnp.broadcast_to(total[None], (N_ZLO, *total.shape))
    half = lax.all_to_all(copies, "col", 0, 0, axis_index_groups=LINES, tiled=True)
    half = half.reshape(chip.shape)
    return lax.all_gather(half, "col", axis=0, axis_index_groups=CHIPS, tiled=True)


def expand_kernel(mask_ref, half_ref, *rest):
    *part_refs, out_ref, held, sems = rest
    rows, width = out_ref.shape
    copies = []
    for start in range(0, width, WIDE):
        factor = jnp.concatenate(
            [part[:, start : start + WIDE] for part in part_refs], axis=0
        )
        full = lax.dot_general(
            half_ref[...],
            factor,
            (((0,), (0,)), ((), ())),
            preferred_element_type=jnp.float32,
        )
        for i in range(rows // TILE):
            for j in range(WIDE // TILE):
                keep = mask_ref[i, start // TILE + j].astype(jnp.float32)
                tile = full[i * TILE : (i + 1) * TILE, j * TILE : (j + 1) * TILE]
                held[pl.ds(i * TILE, TILE), pl.ds(start + j * TILE, TILE)] = (
                    tile * keep
                ).astype(held.dtype)
        done = pl.ds(start, WIDE)
        copy = pltpu.make_async_copy(
            held.at[:, done], out_ref.at[:, done], sems.at[start // WIDE]
        )
        copy.start()
        copies.append(copy)
    for copy in copies:
        copy.wait()


def expand_half(pair_mask, half, parts):
    depth, rows = half.shape
    width = parts[0].shape[1]
    whole = pl.BlockSpec(memory_space=pltpu.VMEM)
    return pl.pallas_call(
        expand_kernel,
        out_shape=jax.ShapeDtypeStruct((rows, width), jnp.bfloat16),
        in_specs=[pl.BlockSpec(memory_space=pltpu.SMEM), whole] + [whole] * len(parts),
        out_specs=pl.BlockSpec(memory_space=pl.ANY),
        scratch_shapes=[
            pltpu.VMEM((rows, width), jnp.bfloat16),
            pltpu.SemaphoreType.DMA((width // WIDE,)),
        ],
        cost_estimate=pl.CostEstimate(
            flops=2 * rows * depth * width,
            bytes_accessed=2 * (rows * depth + depth * width + rows * width),
            transcendentals=0,
        ),
        compiler_params=pltpu.CompilerParams(vmem_limit_bytes=24 * 1024 * 1024),
    )(pair_mask, half, *parts)


def mask_kernel(mask_ref, block_ref, out_ref):
    for j in range(block_ref.shape[1] // TILE):
        cols = pl.ds(j * TILE, TILE)
        keep = mask_ref[0, j].astype(jnp.float32).astype(block_ref.dtype)
        tile = block_ref[:, cols] * keep
        for i in range(out_ref.shape[0]):
            out_ref[i, :, cols] = tile


def masked_copies(factors, factor_mask, count):
    return pl.pallas_call(
        mask_kernel,
        out_shape=jax.ShapeDtypeStruct((count, *factors.shape), factors.dtype),
        in_specs=[
            pl.BlockSpec(memory_space=pltpu.SMEM),
            pl.BlockSpec(memory_space=pltpu.VMEM),
        ],
        out_specs=pl.BlockSpec(memory_space=pltpu.VMEM),
    )(factor_mask, factors)


def body(amplitudes, factors, pair_mask, factor_mask):
    domain = expand_mask(pair_mask, TILE, TILE)
    masked_amps = amplitudes * domain
    block = gather_class(factors, factor_mask)
    block, masked_amps = lax.optimization_barrier((block, masked_amps))
    right = fetch(block, 0, 1)
    left = fetch(block, 0, -1)
    above = fetch(block, -1, 0)
    below = fetch(block, 1, 0)
    far = fetch(right, 0, 1)
    above_right = fetch(right, -1, 0)
    below_right = fetch(right, 1, 0)
    even = [block, left, above, below]
    odd = [right, far, above_right, below_right]
    first = lax.axis_index("col") % N_CORE == 0
    sent = [product(jnp.where(first, o, e), masked_amps) for e, o in zip(even, odd)]
    kept = [product(jnp.where(first, e, o), masked_amps) for e, o in zip(even, odd)]
    sent, kept[0] = lax.optimization_barrier((jnp.concatenate(sent, axis=0), kept[0]))
    kept = jnp.concatenate(kept, axis=0)
    return expand_half(pair_mask, sum_over_columns(sent, kept), even + odd)


def solution(mesh):
    spec = P("row", "col")
    return jax.shard_map(
        body, mesh=mesh, in_specs=(spec,) * 4, out_specs=spec, check_vma=False
    )
```

```python
import jax
import jax.numpy as jnp
from jax import lax
from jax.experimental import pallas as pl
from jax.experimental.pallas import tpu as pltpu
from jax.sharding import PartitionSpec as P

TILE = 128
N_ZHI, N_Y, N_X, N_ZLO, N_CORE = 3, 8, 4, 4, 2
WIDE = 512
CLASS = ((0, 0), (2, 2), (4, 0), (6, 2))
LINES = [[z * N_CORE + c for z in range(N_ZLO)] for c in range(N_CORE)]
CHIPS = [[z * N_CORE + c for c in range(N_CORE)] for z in range(N_ZLO)]


def row_index(z, y, x):
    return (z * N_Y + y % N_Y) * N_X + x % N_X


def class_groups():
    groups, seen = [], set()
    for y in range(N_Y):
        for x in range(N_X):
            group = [
                row_index(z, y + dy, x + dx) for z in range(N_ZHI) for dy, dx in CLASS
            ]
            group.sort()
            if group[0] not in seen:
                seen.add(group[0])
                groups.append(group)
    return groups


def fetch(block, dy, dx):
    pairs = [
        (row_index(z, y + dy, x + dx), row_index(z, y, x))
        for z in range(N_ZHI)
        for y in range(N_Y)
        for x in range(N_X)
    ]
    return lax.ppermute(block, "row", pairs)


def gather_class(factors, factor_mask):
    copies = masked_copies(factors, factor_mask, N_ZHI * len(CLASS))
    got = lax.all_to_all(
        copies, "row", 0, 0, axis_index_groups=class_groups(), tiled=True
    )
    return got.reshape(-1, factors.shape[1])


def product(part, amps):
    return lax.dot_general(
        part, amps, (((1,), (1,)), ((), ())), preferred_element_type=jnp.float32
    )


def sum_over_columns(sent, kept):
    swap = [(z * N_CORE + c, z * N_CORE + 1 - c) for z in range(N_ZLO) for c in (0, 1)]
    chip = (kept + lax.ppermute(sent, "col", swap)).astype(jnp.bfloat16)
    pieces = lax.all_to_all(chip, "col", 0, 0, axis_index_groups=LINES, tiled=True)
    pieces = pieces.reshape(N_ZLO, chip.shape[0] // N_ZLO, -1).astype(jnp.float32)
    total = (pieces[0] + pieces[1] + pieces[2] + pieces[3]).astype(jnp.bfloat16)
    copies = jnp.broadcast_to(total[None], (N_ZLO, *total.shape))
    half = lax.all_to_all(copies, "col", 0, 0, axis_index_groups=LINES, tiled=True)
    half = half.reshape(chip.shape)
    return lax.all_gather(half, "col", axis=0, axis_index_groups=CHIPS, tiled=True)


def expand_kernel(mask_ref, half_ref, *rest):
    *part_refs, out_ref, held, sems = rest
    rows, width = out_ref.shape
    copies = []
    for start in range(0, width, WIDE):
        factor = jnp.concatenate(
            [part[:, start : start + WIDE] for part in part_refs], axis=0
        )
        full = lax.dot_general(
            half_ref[...],
            factor,
            (((0,), (0,)), ((), ())),
            preferred_element_type=jnp.float32,
        )
        for i in range(rows // TILE):
            for j in range(WIDE // TILE):
                keep = mask_ref[i, start // TILE + j].astype(jnp.float32)
                tile = full[i * TILE : (i + 1) * TILE, j * TILE : (j + 1) * TILE]
                held[pl.ds(i * TILE, TILE), pl.ds(start + j * TILE, TILE)] = (
                    tile * keep
                ).astype(held.dtype)
        done = pl.ds(start, WIDE)
        copy = pltpu.make_async_copy(
            held.at[:, done], out_ref.at[:, done], sems.at[start // WIDE]
        )
        copy.start()
        copies.append(copy)
    for copy in copies:
        copy.wait()


def expand_half(pair_mask, half, parts):
    depth, rows = half.shape
    width = parts[0].shape[1]
    whole = pl.BlockSpec(memory_space=pltpu.VMEM)
    return pl.pallas_call(
        expand_kernel,
        out_shape=jax.ShapeDtypeStruct((rows, width), jnp.bfloat16),
        in_specs=[pl.BlockSpec(memory_space=pltpu.SMEM), whole] + [whole] * len(parts),
        out_specs=pl.BlockSpec(memory_space=pl.ANY),
        scratch_shapes=[
            pltpu.VMEM((rows, width), jnp.bfloat16),
            pltpu.SemaphoreType.DMA((width // WIDE,)),
        ],
        cost_estimate=pl.CostEstimate(
            flops=2 * rows * depth * width,
            bytes_accessed=2 * (rows * depth + depth * width + rows * width),
            transcendentals=0,
        ),
        compiler_params=pltpu.CompilerParams(vmem_limit_bytes=24 * 1024 * 1024),
    )(pair_mask, half, *parts)


def mask_kernel(mask_ref, block_ref, out_ref):
    for j in range(block_ref.shape[1] // TILE):
        cols = pl.ds(j * TILE, TILE)
        keep = mask_ref[0, j].astype(jnp.float32).astype(block_ref.dtype)
        tile = block_ref[:, cols] * keep
        for i in range(out_ref.shape[0]):
            out_ref[i, :, cols] = tile


def masked_copies(factors, factor_mask, count):
    return pl.pallas_call(
        mask_kernel,
        out_shape=jax.ShapeDtypeStruct((count, *factors.shape), factors.dtype),
        in_specs=[
            pl.BlockSpec(memory_space=pltpu.SMEM),
            pl.BlockSpec(memory_space=pltpu.VMEM),
        ],
        out_specs=pl.BlockSpec(memory_space=pltpu.VMEM),
    )(factor_mask, factors)


def amps_kernel(mask_ref, amps_ref, out_ref):
    step = pl.program_id(0)
    rows = pl.ds(pl.multiple_of(step * TILE, TILE), TILE)
    for j in range(amps_ref.shape[1] // TILE):
        cols = pl.ds(j * TILE, TILE)
        keep = mask_ref[step, j].astype(jnp.float32).astype(amps_ref.dtype)
        out_ref[rows, cols] = amps_ref[:, cols] * keep


def mask_amps(amplitudes, pair_mask):
    rows, width = amplitudes.shape
    return pl.pallas_call(
        amps_kernel,
        out_shape=jax.ShapeDtypeStruct(amplitudes.shape, amplitudes.dtype),
        grid=(rows // TILE,),
        in_specs=[
            pl.BlockSpec(memory_space=pltpu.SMEM),
            pl.BlockSpec((TILE, width), lambda i: (i, 0)),
        ],
        out_specs=pl.BlockSpec(memory_space=pltpu.VMEM),
        cost_estimate=pl.CostEstimate(
            flops=rows * width, bytes_accessed=4 * rows * width, transcendentals=0
        ),
        compiler_params=pltpu.CompilerParams(vmem_limit_bytes=16 * 1024 * 1024),
    )(pair_mask, amplitudes)


def body(amplitudes, factors, pair_mask, factor_mask):
    masked_amps = mask_amps(amplitudes, pair_mask)
    block = gather_class(factors, factor_mask)
    block, masked_amps = lax.optimization_barrier((block, masked_amps))
    right = fetch(block, 0, 1)
    left = fetch(block, 0, -1)
    above = fetch(block, -1, 0)
    below = fetch(block, 1, 0)
    far = fetch(right, 0, 1)
    above_right = fetch(right, -1, 0)
    below_right = fetch(right, 1, 0)
    even = [block, left, above, below]
    odd = [right, far, above_right, below_right]
    first = lax.axis_index("col") % N_CORE == 0
    sent = [product(jnp.where(first, o, e), masked_amps) for e, o in zip(even, odd)]
    kept = [product(jnp.where(first, e, o), masked_amps) for e, o in zip(even, odd)]
    sent, kept[0] = lax.optimization_barrier((jnp.concatenate(sent, axis=0), kept[0]))
    kept = jnp.concatenate(kept, axis=0)
    return expand_half(pair_mask, sum_over_columns(sent, kept), even + odd)


def solution(mesh):
    spec = P("row", "col")
    return jax.shard_map(
        body, mesh=mesh, in_specs=(spec,) * 4, out_specs=spec, check_vma=False
    )
```

```python
import jax
import jax.numpy as jnp
from jax import lax
from jax.experimental import pallas as pl
from jax.experimental.pallas import tpu as pltpu
from jax.sharding import PartitionSpec as P

TILE = 128
N_ZHI, N_Y, N_X, N_ZLO, N_CORE = 3, 8, 4, 4, 2
WIDE = 512
CLASS = ((0, 0), (2, 2), (4, 0), (6, 2))
LINES = [[z * N_CORE + c for z in range(N_ZLO)] for c in range(N_CORE)]
CHIPS = [[z * N_CORE + c for c in range(N_CORE)] for z in range(N_ZLO)]


def row_index(z, y, x):
    return (z * N_Y + y % N_Y) * N_X + x % N_X


def class_groups():
    groups, seen = [], set()
    for y in range(N_Y):
        for x in range(N_X):
            group = [
                row_index(z, y + dy, x + dx) for z in range(N_ZHI) for dy, dx in CLASS
            ]
            group.sort()
            if group[0] not in seen:
                seen.add(group[0])
                groups.append(group)
    return groups


def fetch(block, dy, dx):
    pairs = [
        (row_index(z, y + dy, x + dx), row_index(z, y, x))
        for z in range(N_ZHI)
        for y in range(N_Y)
        for x in range(N_X)
    ]
    return lax.ppermute(block, "row", pairs)


def gather_class(factors, factor_mask):
    copies = masked_copies(factors, factor_mask, N_ZHI * len(CLASS))
    got = lax.all_to_all(
        copies, "row", 0, 0, axis_index_groups=class_groups(), tiled=True
    )
    return got.reshape(-1, factors.shape[1])


def product(part, amps):
    return lax.dot_general(
        part, amps, (((1,), (1,)), ((), ())), preferred_element_type=jnp.float32
    )


def swap_cores(sent):
    pairs = [(z * N_CORE + c, z * N_CORE + 1 - c) for z in range(N_ZLO) for c in (0, 1)]
    return lax.ppermute(sent, "col", pairs)


def sum_over_lines(chip):
    pieces = lax.all_to_all(chip, "col", 0, 0, axis_index_groups=LINES, tiled=True)
    pieces = pieces.reshape(N_ZLO, chip.shape[0] // N_ZLO, -1).astype(jnp.float32)
    total = (pieces[0] + pieces[1] + pieces[2] + pieces[3]).astype(jnp.bfloat16)
    copies = jnp.broadcast_to(total[None], (N_ZLO, *total.shape))
    half = lax.all_to_all(copies, "col", 0, 0, axis_index_groups=LINES, tiled=True)
    half = half.reshape(chip.shape)
    return lax.all_gather(half, "col", axis=0, axis_index_groups=CHIPS, tiled=True)


def expand_kernel(mask_ref, half_ref, *rest):
    *part_refs, out_ref, held, sems = rest
    rows, width = out_ref.shape
    copies = []
    for start in range(0, width, WIDE):
        factor = jnp.concatenate(
            [part[:, start : start + WIDE] for part in part_refs], axis=0
        )
        full = lax.dot_general(
            half_ref[...],
            factor,
            (((0,), (0,)), ((), ())),
            preferred_element_type=jnp.float32,
        )
        for i in range(rows // TILE):
            for j in range(WIDE // TILE):
                keep = mask_ref[i, start // TILE + j].astype(jnp.float32)
                tile = full[i * TILE : (i + 1) * TILE, j * TILE : (j + 1) * TILE]
                held[pl.ds(i * TILE, TILE), pl.ds(start + j * TILE, TILE)] = (
                    tile * keep
                ).astype(held.dtype)
        done = pl.ds(start, WIDE)
        copy = pltpu.make_async_copy(
            held.at[:, done], out_ref.at[:, done], sems.at[start // WIDE]
        )
        copy.start()
        copies.append(copy)
    for copy in copies:
        copy.wait()


def expand_half(pair_mask, half, parts):
    depth, rows = half.shape
    width = parts[0].shape[1]
    whole = pl.BlockSpec(memory_space=pltpu.VMEM)
    return pl.pallas_call(
        expand_kernel,
        out_shape=jax.ShapeDtypeStruct((rows, width), jnp.bfloat16),
        in_specs=[pl.BlockSpec(memory_space=pltpu.SMEM), whole] + [whole] * len(parts),
        out_specs=pl.BlockSpec(memory_space=pl.ANY),
        scratch_shapes=[
            pltpu.VMEM((rows, width), jnp.bfloat16),
            pltpu.SemaphoreType.DMA((width // WIDE,)),
        ],
        cost_estimate=pl.CostEstimate(
            flops=2 * rows * depth * width,
            bytes_accessed=2 * (rows * depth + depth * width + rows * width),
            transcendentals=0,
        ),
        compiler_params=pltpu.CompilerParams(vmem_limit_bytes=24 * 1024 * 1024),
    )(pair_mask, half, *parts)


def mask_kernel(mask_ref, block_ref, out_ref):
    for j in range(block_ref.shape[1] // TILE):
        cols = pl.ds(j * TILE, TILE)
        keep = mask_ref[0, j].astype(jnp.float32).astype(block_ref.dtype)
        tile = block_ref[:, cols] * keep
        for i in range(out_ref.shape[0]):
            out_ref[i, :, cols] = tile


def masked_copies(factors, factor_mask, count):
    return pl.pallas_call(
        mask_kernel,
        out_shape=jax.ShapeDtypeStruct((count, *factors.shape), factors.dtype),
        in_specs=[
            pl.BlockSpec(memory_space=pltpu.SMEM),
            pl.BlockSpec(memory_space=pltpu.VMEM),
        ],
        out_specs=pl.BlockSpec(memory_space=pltpu.VMEM),
    )(factor_mask, factors)


def amps_kernel(mask_ref, amps_ref, out_ref):
    step = pl.program_id(0)
    rows = pl.ds(pl.multiple_of(step * TILE, TILE), TILE)
    for j in range(amps_ref.shape[1] // TILE):
        cols = pl.ds(j * TILE, TILE)
        keep = mask_ref[step, j].astype(jnp.float32).astype(amps_ref.dtype)
        out_ref[rows, cols] = amps_ref[:, cols] * keep


def mask_amps(amplitudes, pair_mask):
    rows, width = amplitudes.shape
    return pl.pallas_call(
        amps_kernel,
        out_shape=jax.ShapeDtypeStruct(amplitudes.shape, amplitudes.dtype),
        grid=(rows // TILE,),
        in_specs=[
            pl.BlockSpec(memory_space=pltpu.SMEM),
            pl.BlockSpec((TILE, width), lambda i: (i, 0)),
        ],
        out_specs=pl.BlockSpec(memory_space=pltpu.VMEM),
        cost_estimate=pl.CostEstimate(
            flops=rows * width, bytes_accessed=4 * rows * width, transcendentals=0
        ),
        compiler_params=pltpu.CompilerParams(vmem_limit_bytes=16 * 1024 * 1024),
    )(pair_mask, amplitudes)


def body(amplitudes, factors, pair_mask, factor_mask):
    masked_amps = mask_amps(amplitudes, pair_mask)
    block = gather_class(factors, factor_mask)
    block, masked_amps = lax.optimization_barrier((block, masked_amps))
    right = fetch(block, 0, 1)
    left = fetch(block, 0, -1)
    above = fetch(block, -1, 0)
    below = fetch(block, 1, 0)
    far = fetch(right, 0, 1)
    above_right = fetch(right, -1, 0)
    below_right = fetch(right, 1, 0)
    even = [left, block, above, below]
    odd = [far, right, above_right, below_right]
    first = lax.axis_index("col") % N_CORE == 0
    def both(mine, other):
        mine, other = jnp.where(first, mine, other), jnp.where(first, other, mine)
        return product(mine, masked_amps), product(other, masked_amps)

    early = [both(e, o) for e, o in zip(even[1:], odd[1:])]
    kept, sent = [jnp.concatenate(chunks, axis=0) for chunks in zip(*early)]
    chip = (kept + swap_cores(sent)).astype(jnp.bfloat16)
    last, chip = lax.optimization_barrier((odd[0], chip))
    kept, sent = both(even[0], last)
    kept = lax.optimization_barrier(kept)
    chip_last = (kept + swap_cores(sent)).astype(jnp.bfloat16)
    chip = jnp.concatenate([chip_last, chip], axis=0)
    return expand_half(pair_mask, sum_over_lines(chip), even + odd)


def solution(mesh):
    spec = P("row", "col")
    return jax.shard_map(
        body, mesh=mesh, in_specs=(spec,) * 4, out_specs=spec, check_vma=False
    )
```

```python
import jax
import jax.numpy as jnp
from jax import lax
from jax.experimental import pallas as pl
from jax.experimental.pallas import tpu as pltpu
from jax.sharding import PartitionSpec as P

TILE = 128
N_ZHI, N_Y, N_X, N_ZLO, N_CORE = 3, 8, 4, 4, 2
WIDE = 512
CLASS = ((0, 0), (2, 2), (4, 0), (6, 2))
LINES = [[z * N_CORE + c for z in range(N_ZLO)] for c in range(N_CORE)]
CHIPS = [[z * N_CORE + c for c in range(N_CORE)] for z in range(N_ZLO)]


def row_index(z, y, x):
    return (z * N_Y + y % N_Y) * N_X + x % N_X


def class_groups():
    groups, seen = [], set()
    for y in range(N_Y):
        for x in range(N_X):
            group = [
                row_index(z, y + dy, x + dx) for z in range(N_ZHI) for dy, dx in CLASS
            ]
            group.sort()
            if group[0] not in seen:
                seen.add(group[0])
                groups.append(group)
    return groups


def fetch(block, dy, dx):
    pairs = [
        (row_index(z, y + dy, x + dx), row_index(z, y, x))
        for z in range(N_ZHI)
        for y in range(N_Y)
        for x in range(N_X)
    ]
    return lax.ppermute(block, "row", pairs)


def gather_class(factors, factor_mask):
    copies = masked_copies(factors, factor_mask, N_ZHI * len(CLASS))
    got = lax.all_to_all(
        copies, "row", 0, 0, axis_index_groups=class_groups(), tiled=True
    )
    return got.reshape(-1, factors.shape[1])


def product(part, amps):
    return lax.dot_general(
        part, amps, (((1,), (1,)), ((), ())), preferred_element_type=jnp.float32
    )


def swap_cores(sent):
    pairs = [(z * N_CORE + c, z * N_CORE + 1 - c) for z in range(N_ZLO) for c in (0, 1)]
    return lax.ppermute(sent, "col", pairs)


def sum_over_lines(chip):
    pieces = lax.all_to_all(chip, "col", 0, 0, axis_index_groups=LINES, tiled=True)
    pieces = pieces.reshape(N_ZLO, chip.shape[0] // N_ZLO, -1).astype(jnp.float32)
    total = (pieces[0] + pieces[1] + pieces[2] + pieces[3]).astype(jnp.bfloat16)
    copies = jnp.broadcast_to(total[None], (N_ZLO, *total.shape))
    half = lax.all_to_all(copies, "col", 0, 0, axis_index_groups=LINES, tiled=True)
    half = half.reshape(chip.shape)
    return lax.all_gather(half, "col", axis=0, axis_index_groups=CHIPS, tiled=True)


def expand_kernel(mask_ref, half_ref, *rest):
    *part_refs, out_ref, held, sems = rest
    rows, width = out_ref.shape
    copies = []
    for start in range(0, width, WIDE):
        factor = jnp.concatenate(
            [part[:, start : start + WIDE] for part in part_refs], axis=0
        )
        full = lax.dot_general(
            half_ref[...],
            factor,
            (((0,), (0,)), ((), ())),
            preferred_element_type=jnp.float32,
        )
        for i in range(rows // TILE):
            for j in range(WIDE // TILE):
                keep = mask_ref[i, start // TILE + j].astype(jnp.float32)
                tile = full[i * TILE : (i + 1) * TILE, j * TILE : (j + 1) * TILE]
                held[pl.ds(i * TILE, TILE), pl.ds(start + j * TILE, TILE)] = (
                    tile * keep
                ).astype(held.dtype)
        done = pl.ds(start, WIDE)
        copy = pltpu.make_async_copy(
            held.at[:, done], out_ref.at[:, done], sems.at[start // WIDE]
        )
        copy.start()
        copies.append(copy)
    for copy in copies:
        copy.wait()


def expand_half(pair_mask, half, parts):
    depth, rows = half.shape
    width = parts[0].shape[1]
    whole = pl.BlockSpec(memory_space=pltpu.VMEM)
    return pl.pallas_call(
        expand_kernel,
        out_shape=jax.ShapeDtypeStruct((rows, width), jnp.bfloat16),
        in_specs=[pl.BlockSpec(memory_space=pltpu.SMEM), whole] + [whole] * len(parts),
        out_specs=pl.BlockSpec(memory_space=pl.ANY),
        scratch_shapes=[
            pltpu.VMEM((rows, width), jnp.bfloat16),
            pltpu.SemaphoreType.DMA((width // WIDE,)),
        ],
        cost_estimate=pl.CostEstimate(
            flops=2 * rows * depth * width,
            bytes_accessed=2 * (rows * depth + depth * width + rows * width),
            transcendentals=0,
        ),
        compiler_params=pltpu.CompilerParams(vmem_limit_bytes=24 * 1024 * 1024),
    )(pair_mask, half, *parts)


def mask_kernel(mask_ref, block_ref, out_ref):
    for j in range(block_ref.shape[1] // TILE):
        cols = pl.ds(j * TILE, TILE)
        keep = mask_ref[0, j].astype(jnp.float32).astype(block_ref.dtype)
        tile = block_ref[:, cols] * keep
        for i in range(out_ref.shape[0]):
            out_ref[i, :, cols] = tile


def masked_copies(factors, factor_mask, count):
    return pl.pallas_call(
        mask_kernel,
        out_shape=jax.ShapeDtypeStruct((count, *factors.shape), factors.dtype),
        in_specs=[
            pl.BlockSpec(memory_space=pltpu.SMEM),
            pl.BlockSpec(memory_space=pltpu.VMEM),
        ],
        out_specs=pl.BlockSpec(memory_space=pltpu.VMEM),
    )(factor_mask, factors)


def amps_kernel(mask_ref, amps_ref, out_ref):
    step = pl.program_id(0)
    rows = pl.ds(pl.multiple_of(step * TILE, TILE), TILE)
    for j in range(amps_ref.shape[1] // TILE):
        cols = pl.ds(j * TILE, TILE)
        keep = mask_ref[step, j].astype(jnp.float32).astype(amps_ref.dtype)
        out_ref[rows, cols] = amps_ref[:, cols] * keep


def mask_amps(amplitudes, pair_mask):
    rows, width = amplitudes.shape
    return pl.pallas_call(
        amps_kernel,
        out_shape=jax.ShapeDtypeStruct(amplitudes.shape, amplitudes.dtype),
        grid=(rows // TILE,),
        in_specs=[
            pl.BlockSpec(memory_space=pltpu.SMEM),
            pl.BlockSpec((TILE, width), lambda i: (i, 0)),
        ],
        out_specs=pl.BlockSpec(memory_space=pltpu.VMEM),
        cost_estimate=pl.CostEstimate(
            flops=rows * width, bytes_accessed=4 * rows * width, transcendentals=0
        ),
        compiler_params=pltpu.CompilerParams(vmem_limit_bytes=16 * 1024 * 1024),
    )(pair_mask, amplitudes)


def body(amplitudes, factors, pair_mask, factor_mask):
    masked_amps = mask_amps(amplitudes, pair_mask)
    block = gather_class(factors, factor_mask)
    block, masked_amps = lax.optimization_barrier((block, masked_amps))
    right = fetch(block, 0, 1)
    left = fetch(block, 0, -1)
    above = fetch(block, -1, 0)
    below = fetch(block, 1, 0)
    far = fetch(right, 0, 1)
    above_right = fetch(right, -1, 0)
    below_right = fetch(right, 1, 0)
    even = [left, above, block, below]
    odd = [far, above_right, right, below_right]
    first = lax.axis_index("col") % N_CORE == 0

    def both(mine, other):
        mine, other = jnp.where(first, mine, other), jnp.where(first, other, mine)
        return product(mine, masked_amps), product(other, masked_amps)

    early = [both(e, o) for e, o in zip(even[2:], odd[2:])]
    kept, sent = [jnp.concatenate(chunks, axis=0) for chunks in zip(*early)]
    chip = (kept + swap_cores(sent)).astype(jnp.bfloat16)
    middle = both(even[1], odd[1])
    last, middle, chip = lax.optimization_barrier((far, middle, chip))
    late = [both(left, last), middle]
    kept, sent = [jnp.concatenate(chunks, axis=0) for chunks in zip(*late)]
    kept = lax.optimization_barrier(kept)
    chip_late = (kept + swap_cores(sent)).astype(jnp.bfloat16)
    chip = jnp.concatenate([chip_late, chip], axis=0)
    return expand_half(pair_mask, sum_over_lines(chip), even + odd)


def solution(mesh):
    spec = P("row", "col")
    return jax.shard_map(
        body, mesh=mesh, in_specs=(spec,) * 4, out_specs=spec, check_vma=False
    )
```

```python
import jax
import jax.numpy as jnp
from jax import lax
from jax.experimental import pallas as pl
from jax.experimental.pallas import tpu as pltpu
from jax.sharding import PartitionSpec as P

TILE = 128
N_ZHI, N_Y, N_X, N_ZLO, N_CORE = 3, 8, 4, 4, 2
WIDE = 512
CLASS = ((0, 0), (2, 2), (4, 0), (6, 2))
CHIPS = [[z * N_CORE + c for c in range(N_CORE)] for z in range(N_ZLO)]


def row_index(z, y, x):
    return (z * N_Y + y % N_Y) * N_X + x % N_X


def class_groups():
    groups, seen = [], set()
    for y in range(N_Y):
        for x in range(N_X):
            group = [
                row_index(z, y + dy, x + dx) for z in range(N_ZHI) for dy, dx in CLASS
            ]
            group.sort()
            if group[0] not in seen:
                seen.add(group[0])
                groups.append(group)
    return groups


def fetch(block, dy, dx):
    pairs = [
        (row_index(z, y + dy, x + dx), row_index(z, y, x))
        for z in range(N_ZHI)
        for y in range(N_Y)
        for x in range(N_X)
    ]
    return lax.ppermute(block, "row", pairs)


def gather_class(factors, factor_mask):
    copies = masked_copies(factors, factor_mask, N_ZHI * len(CLASS))
    got = lax.all_to_all(
        copies, "row", 0, 0, axis_index_groups=class_groups(), tiled=True
    )
    return got.reshape(-1, factors.shape[1])


def product(part, amps):
    return lax.dot_general(
        part, amps, (((1,), (1,)), ((), ())), preferred_element_type=jnp.float32
    )


def swap_cores(sent):
    pairs = [(z * N_CORE + c, z * N_CORE + 1 - c) for z in range(N_ZLO) for c in (0, 1)]
    return lax.ppermute(sent, "col", pairs)


def along_line(piece, by):
    pairs = [
        (z * N_CORE + c, (z + by) % N_ZLO * N_CORE + c)
        for z in range(N_ZLO)
        for c in range(N_CORE)
    ]
    return lax.ppermute(piece, "col", pairs)


def sum_over_lines(chip):
    pieces = chip.reshape(N_ZLO, chip.shape[0] // N_ZLO, -1)
    place = lax.axis_index("col") // N_CORE
    far_first = (2, 1, 3)

    def piece(by):
        return lax.dynamic_index_in_dim(pieces, (place + by) % N_ZLO, 0, False)

    got = [along_line(piece(by), by) for by in far_first]
    total = piece(0).astype(jnp.float32)
    for other in got:
        total = total + other.astype(jnp.float32)
    total = total.astype(jnp.bfloat16)
    half = jnp.zeros(pieces.shape, jnp.bfloat16)
    half = lax.dynamic_update_index_in_dim(half, total, place, 0)
    for by in far_first:
        source = (place - by) % N_ZLO
        half = lax.dynamic_update_index_in_dim(half, along_line(total, by), source, 0)
    half = half.reshape(chip.shape)
    return lax.all_gather(half, "col", axis=0, axis_index_groups=CHIPS, tiled=True)


def expand_kernel(mask_ref, half_ref, *rest):
    *part_refs, out_ref, held, sems = rest
    rows, width = out_ref.shape
    copies = []
    for start in range(0, width, WIDE):
        factor = jnp.concatenate(
            [part[:, start : start + WIDE] for part in part_refs], axis=0
        )
        full = lax.dot_general(
            half_ref[...],
            factor,
            (((0,), (0,)), ((), ())),
            preferred_element_type=jnp.float32,
        )
        for i in range(rows // TILE):
            for j in range(WIDE // TILE):
                keep = mask_ref[i, start // TILE + j].astype(jnp.float32)
                tile = full[i * TILE : (i + 1) * TILE, j * TILE : (j + 1) * TILE]
                held[pl.ds(i * TILE, TILE), pl.ds(start + j * TILE, TILE)] = (
                    tile * keep
                ).astype(held.dtype)
        done = pl.ds(start, WIDE)
        copy = pltpu.make_async_copy(
            held.at[:, done], out_ref.at[:, done], sems.at[start // WIDE]
        )
        copy.start()
        copies.append(copy)
    for copy in copies:
        copy.wait()


def expand_half(pair_mask, half, parts):
    depth, rows = half.shape
    width = parts[0].shape[1]
    whole = pl.BlockSpec(memory_space=pltpu.VMEM)
    return pl.pallas_call(
        expand_kernel,
        out_shape=jax.ShapeDtypeStruct((rows, width), jnp.bfloat16),
        in_specs=[pl.BlockSpec(memory_space=pltpu.SMEM), whole] + [whole] * len(parts),
        out_specs=pl.BlockSpec(memory_space=pl.ANY),
        scratch_shapes=[
            pltpu.VMEM((rows, width), jnp.bfloat16),
            pltpu.SemaphoreType.DMA((width // WIDE,)),
        ],
        cost_estimate=pl.CostEstimate(
            flops=2 * rows * depth * width,
            bytes_accessed=2 * (rows * depth + depth * width + rows * width),
            transcendentals=0,
        ),
        compiler_params=pltpu.CompilerParams(vmem_limit_bytes=24 * 1024 * 1024),
    )(pair_mask, half, *parts)


def mask_kernel(mask_ref, block_ref, out_ref):
    for j in range(block_ref.shape[1] // TILE):
        cols = pl.ds(j * TILE, TILE)
        keep = mask_ref[0, j].astype(jnp.float32).astype(block_ref.dtype)
        tile = block_ref[:, cols] * keep
        for i in range(out_ref.shape[0]):
            out_ref[i, :, cols] = tile


def masked_copies(factors, factor_mask, count):
    return pl.pallas_call(
        mask_kernel,
        out_shape=jax.ShapeDtypeStruct((count, *factors.shape), factors.dtype),
        in_specs=[
            pl.BlockSpec(memory_space=pltpu.SMEM),
            pl.BlockSpec(memory_space=pltpu.VMEM),
        ],
        out_specs=pl.BlockSpec(memory_space=pltpu.VMEM),
    )(factor_mask, factors)


def amps_kernel(mask_ref, amps_ref, out_ref):
    step = pl.program_id(0)
    rows = pl.ds(pl.multiple_of(step * TILE, TILE), TILE)
    for j in range(amps_ref.shape[1] // TILE):
        cols = pl.ds(j * TILE, TILE)
        keep = mask_ref[step, j].astype(jnp.float32).astype(amps_ref.dtype)
        out_ref[rows, cols] = amps_ref[:, cols] * keep


def mask_amps(amplitudes, pair_mask):
    rows, width = amplitudes.shape
    return pl.pallas_call(
        amps_kernel,
        out_shape=jax.ShapeDtypeStruct(amplitudes.shape, amplitudes.dtype),
        grid=(rows // TILE,),
        in_specs=[
            pl.BlockSpec(memory_space=pltpu.SMEM),
            pl.BlockSpec((TILE, width), lambda i: (i, 0)),
        ],
        out_specs=pl.BlockSpec(memory_space=pltpu.VMEM),
        cost_estimate=pl.CostEstimate(
            flops=rows * width, bytes_accessed=4 * rows * width, transcendentals=0
        ),
        compiler_params=pltpu.CompilerParams(vmem_limit_bytes=16 * 1024 * 1024),
    )(pair_mask, amplitudes)


def body(amplitudes, factors, pair_mask, factor_mask):
    masked_amps = mask_amps(amplitudes, pair_mask)
    block = gather_class(factors, factor_mask)
    block, masked_amps = lax.optimization_barrier((block, masked_amps))
    right = fetch(block, 0, 1)
    left = fetch(block, 0, -1)
    above = fetch(block, -1, 0)
    below = fetch(block, 1, 0)
    far = fetch(right, 0, 1)
    above_right = fetch(right, -1, 0)
    below_right = fetch(right, 1, 0)
    even = [left, above, block, below]
    odd = [far, above_right, right, below_right]
    first = lax.axis_index("col") % N_CORE == 0

    def both(mine, other):
        mine, other = jnp.where(first, mine, other), jnp.where(first, other, mine)
        return product(mine, masked_amps), product(other, masked_amps)

    early = [both(e, o) for e, o in zip(even[2:], odd[2:])]
    kept, sent = [jnp.concatenate(chunks, axis=0) for chunks in zip(*early)]
    chip = (kept + swap_cores(sent)).astype(jnp.bfloat16)
    middle = both(even[1], odd[1])
    last, middle, chip = lax.optimization_barrier((far, middle, chip))
    late = [both(left, last), middle]
    kept, sent = [jnp.concatenate(chunks, axis=0) for chunks in zip(*late)]
    kept = lax.optimization_barrier(kept)
    chip_late = (kept + swap_cores(sent)).astype(jnp.bfloat16)
    chip = jnp.concatenate([chip_late, chip], axis=0)
    return expand_half(pair_mask, sum_over_lines(chip), even + odd)


def solution(mesh):
    spec = P("row", "col")
    return jax.shard_map(
        body, mesh=mesh, in_specs=(spec,) * 4, out_specs=spec, check_vma=False
    )
```

```python
import jax
import jax.numpy as jnp
from jax import lax
from jax.experimental import pallas as pl
from jax.experimental.pallas import tpu as pltpu
from jax.sharding import PartitionSpec as P

TILE = 128
N_ZHI, N_Y, N_X, N_ZLO, N_CORE = 3, 8, 4, 4, 2
WIDE = 512
CLASS = ((0, 0), (2, 2), (4, 0), (6, 2))
LINES = [[z * N_CORE + c for z in range(N_ZLO)] for c in range(N_CORE)]
CHIPS = [[z * N_CORE + c for c in range(N_CORE)] for z in range(N_ZLO)]


def row_index(z, y, x):
    return (z * N_Y + y % N_Y) * N_X + x % N_X


def class_groups():
    groups, seen = [], set()
    for y in range(N_Y):
        for x in range(N_X):
            group = [
                row_index(z, y + dy, x + dx) for z in range(N_ZHI) for dy, dx in CLASS
            ]
            group.sort()
            if group[0] not in seen:
                seen.add(group[0])
                groups.append(group)
    return groups


def fetch(block, dy, dx):
    pairs = [
        (row_index(z, y + dy, x + dx), row_index(z, y, x))
        for z in range(N_ZHI)
        for y in range(N_Y)
        for x in range(N_X)
    ]
    return lax.ppermute(block, "row", pairs)


def gather_class(factors, factor_mask):
    copies = masked_copies(factors, factor_mask, N_ZHI * len(CLASS))
    got = lax.all_to_all(
        copies, "row", 0, 0, axis_index_groups=class_groups(), tiled=True
    )
    return got.reshape(-1, factors.shape[1])


def product(part, amps):
    return lax.dot_general(
        part, amps, (((1,), (1,)), ((), ())), preferred_element_type=jnp.float32
    )


def swap_cores(sent):
    pairs = [(z * N_CORE + c, z * N_CORE + 1 - c) for z in range(N_ZLO) for c in (0, 1)]
    return lax.ppermute(sent, "col", pairs)


def sum_over_lines(chip):
    pieces = lax.all_to_all(chip, "col", 0, 0, axis_index_groups=LINES, tiled=True)
    pieces = pieces.reshape(N_ZLO, chip.shape[0] // N_ZLO, -1).astype(jnp.float32)
    total = (pieces[0] + pieces[1] + pieces[2] + pieces[3]).astype(jnp.bfloat16)
    copies = jnp.broadcast_to(total[None], (N_ZLO, *total.shape))
    half = lax.all_to_all(copies, "col", 0, 0, axis_index_groups=LINES, tiled=True)
    half = half.reshape(chip.shape)
    return lax.all_gather(half, "col", axis=0, axis_index_groups=CHIPS, tiled=True)


def expand_kernel(mask_ref, half_ref, *rest):
    *part_refs, out_ref, held, sems = rest
    rows, width = out_ref.shape
    copies = []
    for start in range(0, width, WIDE):
        factor = jnp.concatenate(
            [part[:, start : start + WIDE] for part in part_refs], axis=0
        )
        full = lax.dot_general(
            half_ref[...],
            factor,
            (((0,), (0,)), ((), ())),
            preferred_element_type=jnp.float32,
        )
        for i in range(rows // TILE):
            for j in range(WIDE // TILE):
                keep = mask_ref[i, start // TILE + j].astype(jnp.float32)
                tile = full[i * TILE : (i + 1) * TILE, j * TILE : (j + 1) * TILE]
                held[pl.ds(i * TILE, TILE), pl.ds(start + j * TILE, TILE)] = (
                    tile * keep
                ).astype(held.dtype)
        done = pl.ds(start, WIDE)
        copy = pltpu.make_async_copy(
            held.at[:, done], out_ref.at[:, done], sems.at[start // WIDE]
        )
        copy.start()
        copies.append(copy)
    for copy in copies:
        copy.wait()


def expand_half(pair_mask, half, parts):
    depth, rows = half.shape
    width = parts[0].shape[1]
    whole = pl.BlockSpec(memory_space=pltpu.VMEM)
    return pl.pallas_call(
        expand_kernel,
        out_shape=jax.ShapeDtypeStruct((rows, width), jnp.bfloat16),
        in_specs=[pl.BlockSpec(memory_space=pltpu.SMEM), whole] + [whole] * len(parts),
        out_specs=pl.BlockSpec(memory_space=pl.ANY),
        scratch_shapes=[
            pltpu.VMEM((rows, width), jnp.bfloat16),
            pltpu.SemaphoreType.DMA((width // WIDE,)),
        ],
        cost_estimate=pl.CostEstimate(
            flops=2 * rows * depth * width,
            bytes_accessed=2 * (rows * depth + depth * width + rows * width),
            transcendentals=0,
        ),
        compiler_params=pltpu.CompilerParams(vmem_limit_bytes=24 * 1024 * 1024),
    )(pair_mask, half, *parts)


def mask_kernel(mask_ref, block_ref, out_ref):
    for j in range(block_ref.shape[1] // TILE):
        cols = pl.ds(j * TILE, TILE)
        keep = mask_ref[0, j].astype(jnp.float32).astype(block_ref.dtype)
        tile = block_ref[:, cols] * keep
        for i in range(out_ref.shape[0]):
            out_ref[i, :, cols] = tile


def masked_copies(factors, factor_mask, count):
    return pl.pallas_call(
        mask_kernel,
        out_shape=jax.ShapeDtypeStruct((count, *factors.shape), factors.dtype),
        in_specs=[
            pl.BlockSpec(memory_space=pltpu.SMEM),
            pl.BlockSpec(memory_space=pltpu.VMEM),
        ],
        out_specs=pl.BlockSpec(memory_space=pltpu.VMEM),
    )(factor_mask, factors)


def amps_kernel(mask_ref, amps_ref, out_ref):
    step = pl.program_id(0)
    rows = pl.ds(pl.multiple_of(step * TILE, TILE), TILE)
    for j in range(amps_ref.shape[1] // TILE):
        cols = pl.ds(j * TILE, TILE)
        keep = mask_ref[step, j].astype(jnp.float32).astype(amps_ref.dtype)
        out_ref[rows, cols] = amps_ref[:, cols] * keep


def mask_amps(amplitudes, pair_mask):
    rows, width = amplitudes.shape
    return pl.pallas_call(
        amps_kernel,
        out_shape=jax.ShapeDtypeStruct(amplitudes.shape, amplitudes.dtype),
        grid=(rows // TILE,),
        in_specs=[
            pl.BlockSpec(memory_space=pltpu.SMEM),
            pl.BlockSpec((TILE, width), lambda i: (i, 0)),
        ],
        out_specs=pl.BlockSpec(memory_space=pltpu.VMEM),
        cost_estimate=pl.CostEstimate(
            flops=rows * width, bytes_accessed=4 * rows * width, transcendentals=0
        ),
        compiler_params=pltpu.CompilerParams(vmem_limit_bytes=16 * 1024 * 1024),
    )(pair_mask, amplitudes)


def body(amplitudes, factors, pair_mask, factor_mask):
    masked_amps = mask_amps(amplitudes, pair_mask)
    block = gather_class(factors, factor_mask)
    block, masked_amps = lax.optimization_barrier((block, masked_amps))
    right = fetch(block, 0, 1)
    left = fetch(block, 0, -1)
    above = fetch(block, -1, 0)
    below = fetch(block, 1, 0)
    far = fetch(right, 0, 1)
    above_right = fetch(right, -1, 0)
    below_right = fetch(right, 1, 0)
    even = [left, above, block, below]
    odd = [far, above_right, right, below_right]
    first = lax.axis_index("col") % N_CORE == 0

    def both(mine, other):
        mine, other = jnp.where(first, mine, other), jnp.where(first, other, mine)
        return product(mine, masked_amps), product(other, masked_amps)

    early = [both(e, o) for e, o in zip(even[2:], odd[2:])]
    kept, sent = [list(chunks) for chunks in zip(*early)]
    amps, _ = lax.optimization_barrier((masked_amps, below))
    kept[0] = product(jnp.where(first, even[2], odd[2]), amps)
    kept, sent = jnp.concatenate(kept, axis=0), jnp.concatenate(sent, axis=0)
    chip = (kept + swap_cores(sent)).astype(jnp.bfloat16)
    middle = both(even[1], odd[1])
    last, middle, chip = lax.optimization_barrier((far, middle, chip))
    late = [both(left, last), middle]
    kept, sent = [jnp.concatenate(chunks, axis=0) for chunks in zip(*late)]
    kept = lax.optimization_barrier(kept)
    chip_late = (kept + swap_cores(sent)).astype(jnp.bfloat16)
    chip = jnp.concatenate([chip_late, chip], axis=0)
    return expand_half(pair_mask, sum_over_lines(chip), even + odd)


def solution(mesh):
    spec = P("row", "col")
    return jax.shard_map(
        body, mesh=mesh, in_specs=(spec,) * 4, out_specs=spec, check_vma=False
    )
```
